32 devices in a mesh: dp: 16 (over z, y, x), space: 2 (over core).
Axes of the slice: x: 2, y: 2, z: 4, core: 2. Of those that a mesh axis runs over, the one named last changes fastest.
Arguments:
- image: bfloat16 [16, 8, 8, 8, 128], P('dp', 'space'), may hold values from -30 to 30
- cotangent: bfloat16 [16, 8, 8, 8, 128], P('dp', 'space'), may hold values from -30 to 30
- first_weight: bfloat16 [3456, 128], P('dp'), may hold values from -0.109375 to 0.109375
- second_weight: bfloat16 [3456, 128], P('dp'), may hold values from -0.109375 to 0.109375
Outputs:
- output: bfloat16 [16, 8, 8, 8, 128], P('dp', 'space')
- image_grad: bfloat16 [16, 8, 8, 8, 128], P('dp', 'space')
- first_grad: float32 [3456, 128], P('dp')
- second_grad: float32 [3456, 128], P('dp')
The draws below stay inside these ranges and needn't reach their ends.
All inputs are finite; a program needn't handle non-finite values.
Results may differ from the reference program's by a relative error of at most 0.013.
Values may be sent and summed in bfloat16 or wider, within the bound.
A program may use at most 64 MiB of HBM per device.

```python
import math
import jax
import jax.numpy as jnp
from jax import lax

C = 128
HEIGHT = 8
WIDTH = 8
ROWS = 3456
DEPTH = 8
PATCHES = 16


def depth_ramp(start, finish):
    place = jnp.arange(DEPTH, dtype=jnp.float32) / (DEPTH - 1)
    return (start + (finish - start) * place).reshape(1, DEPTH, 1, 1, 1)


def rough_field(key, start, finish, offset):
    first, second, third = jax.random.split(key, 3)
    shape = (PATCHES, DEPTH, HEIGHT, WIDTH, C)
    base = jax.random.truncated_normal(first, -4.0, 4.0, shape, jnp.float32)
    ramp = depth_ramp(start, finish)
    scales = jnp.exp(jax.random.uniform(second, (C,), jnp.float32, -0.5, 0.5))
    signs = jax.random.uniform(third, (C,), jnp.float32, -1.0, 1.0)
    return ramp * (base * scales + offset * signs)


def draw_image(key, part):
    return rough_field(jax.random.fold_in(key, 11), 1.0, 3.0, 0.5).astype(jnp.bfloat16)


def draw_cotangent(key, part):
    return rough_field(jax.random.fold_in(key, 23), 1.0, 3.0, 0.2).astype(jnp.bfloat16)


def levels(stream_key, extent, cuts, least, high):
    def one(position, shards_of):
        heights = jax.random.uniform(jax.random.fold_in(jax.random.fold_in(stream_key, 6), position), (shards_of,), jnp.float32, least / len(cuts), high / len(cuts))
        return jnp.repeat(jnp.exp(heights), extent[position] // shards_of).reshape((-1,) + (1,) * (len(extent) - position - 1))

    factor_of = one(*cuts[0])
    for cut in cuts[1:]:
        factor_of = factor_of * one(*cut)
    return factor_of


def bell_draw(key, dims, scale, bound, shards=(), kind=jnp.bfloat16):
    loudness = levels(key, dims, shards, -0.22, 0.18) if shards else 1.0
    array = jax.random.normal(key, dims, jnp.float32) * scale * loudness
    return jnp.minimum(jnp.maximum(array, -bound), bound).astype(kind)


def setup_inputs(seed: int = 0) -> dict:
    key_of = jax.random.split(jax.random.key(seed), 5)
    return {
        "image": draw_image(jax.random.fold_in(key_of[4], 71), 0),
        "cotangent": draw_cotangent(jax.random.fold_in(key_of[4], 71), 0),
        "first_weight": bell_draw(key_of[2], (ROWS, C), ROWS ** -0.5, 0.109375, ((0, 16),)),
        "second_weight": bell_draw(key_of[3], (ROWS, C), ROWS ** -0.5, 0.109375, ((0, 16),)),
    }


EPSILON = 1e-05

def gelu_value(values):
    return 0.5 * values * (1.0 + lax.erf(values * 0.7071067811865476))

def gelu_slope(values):
    return 0.5 * (1.0 + lax.erf(values * 0.7071067811865476)) + values * jnp.exp(-0.5 * values * values) * 0.3989422804014327

def product(left, right):
    return jnp.dot(left.astype(jnp.float32), right.astype(jnp.float32), precision=lax.Precision.HIGHEST)

def columns(volume):
    depth, height, width, channels = volume.shape
    padded = jnp.pad(volume, ((1, 1), (1, 1), (1, 1), (0, 0)))
    pieces = [padded[first:first + depth, second:second + height, third:third + width, :] for first in range(3) for second in range(3) for third in range(3)]
    return jnp.concatenate(pieces, axis=-1).reshape(depth * height * width, 27 * channels)

def reverse_taps(weight):
    channels = weight.shape[1]
    return weight.reshape(27, channels, channels)[::-1].transpose(0, 2, 1).reshape(27 * channels, channels)

def normalize(values):
    average = lax.optimization_barrier(jnp.mean(values, axis=0))
    square_mean = lax.optimization_barrier(jnp.mean(values * values, axis=0))
    inverse = lax.rsqrt(square_mean - average * average + EPSILON)
    return ((values - average) * inverse, inverse)

def norm_back(grad, normed, inverse):
    return inverse * (grad - lax.optimization_barrier(jnp.mean(grad, axis=0)) - normed * lax.optimization_barrier(jnp.mean(grad * normed, axis=0)))

def reference(image, cotangent, first_weight, second_weight):
    shape = image.shape[1:]
    cells = shape[0] * shape[1] * shape[2]

    def one_patch(carry, item):
        volume, outer = item
        first_columns = columns(volume)
        first_norm, first_inverse = normalize(product(first_columns, first_weight))
        hidden = gelu_value(first_norm).astype(jnp.bfloat16)
        second_columns = columns(hidden.reshape(shape))
        second_norm, second_inverse = normalize(product(second_columns, second_weight))
        summed = volume.reshape(cells, C).astype(jnp.float32) + second_norm
        output = gelu_value(summed).astype(jnp.bfloat16)
        outer_grad = outer.reshape(cells, C).astype(jnp.float32) * gelu_slope(summed)
        second_delta = norm_back(outer_grad, second_norm, second_inverse).astype(jnp.bfloat16)
        second_part = product(second_columns.T, second_delta)
        inner_grad = product(columns(second_delta.reshape(shape)), reverse_taps(second_weight))
        first_delta = norm_back(inner_grad * gelu_slope(first_norm), first_norm, first_inverse).astype(jnp.bfloat16)
        first_part = product(first_columns.T, first_delta)
        image_grad = (outer_grad + product(columns(first_delta.reshape(shape)), reverse_taps(first_weight))).astype(jnp.bfloat16)
        return ((carry[0] + first_part, carry[1] + second_part), (output.reshape(shape), image_grad.reshape(shape)))
    zeros = jnp.zeros((ROWS, C), jnp.float32)
    totals, results = lax.scan(one_patch, (zeros, zeros), (image, cotangent))
    factor = 1.0 / math.sqrt(PATCHES * DEPTH * HEIGHT * WIDTH)
    return (results[0], results[1], totals[0] * factor, totals[1] * factor)
```

```python
import functools
import math

import jax
import jax.numpy as jnp
from jax import lax
from jax.experimental import pallas as pl
from jax.experimental.pallas import tpu as pltpu
from jax.sharding import PartitionSpec as P

MESH = pl.DeviceIdType.MESH

EPSILON = 1e-05


def with_halo(cells, sides, width):
    for axis, dim in sides:
        count = lax.axis_size(axis)
        ends = count - 1
        head = lax.slice_in_dim(cells, 0, width, axis=dim)
        tail = lax.slice_in_dim(cells, cells.shape[dim] - width, cells.shape[dim], axis=dim)
        cells = jnp.concatenate(
            [
                lax.ppermute(tail, axis, [(i, (i + 1) % count) for i in range(ends)]),
                cells,
                lax.ppermute(head, axis, [((i + 1) % count, i) for i in range(ends)]),
            ],
            axis=dim,
        )
    return cells


def gelu_value(values):
    return 0.5 * values * (1.0 + lax.erf(values * 0.7071067811865476))


def gelu_slope(values):
    return (
        0.5 * (1.0 + lax.erf(values * 0.7071067811865476))
        + values * jnp.exp(-0.5 * values * values) * 0.3989422804014327
    )


def columns(deep):
    depth = deep.shape[0] - 2
    height, width, channels = (deep.shape[1], deep.shape[2], deep.shape[3])
    padded = jnp.pad(deep, ((0, 0), (1, 1), (1, 1), (0, 0)))
    pieces = [
        padded[first : first + depth, second : second + height, third : third + width, :]
        for first in range(3)
        for second in range(3)
        for third in range(3)
    ]
    return jnp.concatenate(pieces, axis=-1).reshape(depth * height * width, 27 * channels)


def reverse_taps(weight):
    channels = weight.shape[1]
    return (
        weight.reshape(27, channels, channels)[::-1]
        .transpose(0, 2, 1)
        .reshape(27 * channels, channels)
    )


def local(image, cotangent, first_weight, second_weight):
    slab = image[0]
    depth, height, width, channels = slab.shape
    cells = depth * height * width
    patch_cells = cells * lax.axis_size("space")
    factor = 1.0 / math.sqrt(patch_cells * lax.axis_size("dp"))

    def unfold_slab(volume):
        deep = with_halo(volume, (("space", 0),), 1)
        return columns(deep)

    def normalize(values):
        totals, squares = lax.psum(
            (jnp.sum(values, axis=0), jnp.sum(values * values, axis=0)), "space"
        )
        average = totals / patch_cells
        inverse = lax.rsqrt(squares / patch_cells - average * average + EPSILON)
        return ((values - average) * inverse, inverse)

    def norm_back(grad, normed, inverse):
        plain_total, paired_total = lax.psum(
            (jnp.sum(grad, axis=0), jnp.sum(grad * normed, axis=0)), "space"
        )
        return inverse * (grad - plain_total / patch_cells - normed * (paired_total / patch_cells))

    def apply_weight(unfolded, shard):
        whole = lax.all_gather(shard, "dp", axis=0, tiled=True)
        return (jnp.dot(unfolded, whole, preferred_element_type=jnp.float32), shard)

    def weight_again(kept):
        whole = lax.all_gather(kept, "dp", axis=0, tiled=True)
        return reverse_taps(whole)

    def reduce_grad(unfolded, delta):
        own_rows = lax.psum_scatter(
            lax.dot_general(
                unfolded, delta, (((0,), (0,)), ((), ())), preferred_element_type=jnp.float32
            ),
            "dp",
            scatter_dimension=0,
            tiled=True,
        )
        return lax.psum(own_rows, "space")

    first_columns = unfold_slab(slab)
    first_conv, first_kept = apply_weight(first_columns, first_weight)
    first_norm, first_inverse = normalize(first_conv)
    hidden = gelu_value(first_norm).astype(jnp.bfloat16)
    second_columns = unfold_slab(hidden.reshape(depth, height, width, channels))
    second_conv, second_kept = apply_weight(second_columns, second_weight)
    second_norm, second_inverse = normalize(second_conv)
    summed = slab.reshape(cells, channels).astype(jnp.float32) + second_norm
    output = gelu_value(summed).astype(jnp.bfloat16)
    outer_grad = cotangent[0].reshape(cells, channels).astype(jnp.float32) * gelu_slope(summed)
    second_delta = norm_back(outer_grad, second_norm, second_inverse).astype(jnp.bfloat16)
    second_grad = reduce_grad(second_columns, second_delta)
    inner_grad = jnp.dot(
        unfold_slab(second_delta.reshape(depth, height, width, channels)),
        weight_again(second_kept),
        preferred_element_type=jnp.float32,
    )
    first_delta = norm_back(inner_grad * gelu_slope(first_norm), first_norm, first_inverse).astype(
        jnp.bfloat16
    )
    first_grad = reduce_grad(first_columns, first_delta)
    backward_term = jnp.dot(
        unfold_slab(first_delta.reshape(depth, height, width, channels)),
        weight_again(first_kept),
        preferred_element_type=jnp.float32,
    )
    image_grad = (outer_grad + backward_term).astype(jnp.bfloat16)
    return (
        output.reshape(image.shape),
        image_grad.reshape(image.shape),
        first_grad * factor,
        second_grad * factor,
    )


def group_size(count):
    size = 1
    while size * size < count and count % (2 * size) == 0:
        size *= 2
    return size


def remote(src, dst, send_sem, recv_sem, device):
    return pltpu.make_async_remote_copy(
        src_ref=src,
        dst_ref=dst,
        send_sem=send_sem,
        recv_sem=recv_sem,
        device_id=device,
        device_id_type=MESH,
    )


def block_kernel(
    sizes,
    image_ref,
    cotangent_ref,
    first_ref,
    second_ref,
    output_ref,
    image_grad_ref,
    first_grad_ref,
    second_grad_ref,
    fields,
    gathered,
    rows_f32,
    weights,
    turned,
    image_cols,
    hidden_cols,
    delta_cols,
    planes,
    grad_rows,
    grad_send,
    grad_recv,
    line_send,
    line_recv,
    halves,
    summed_ref,
    outer_ref,
    field_send,
    field_recv,
    line_ws,
    line_wr,
    plane_ws,
    plane_wr,
    core_ws,
    core_wr,
    plane_gs,
    plane_gr,
    line_gs,
    line_gr,
    core_gs,
    core_gr,
):
    count, inner, depth, height, width, channels, rows = sizes
    outer = count // inner
    half = gathered.shape[3]
    cells = depth * height * width
    own_cells = cells // 2
    area = height * width
    factor = 1.0 / math.sqrt(cells * count)
    me = lax.axis_index("dp")
    core = lax.axis_index("space")
    z = lax.div(me, inner)
    p = lax.rem(me, inner)
    sibling = (me, 1 - core)

    def line_peer(s):
        return lax.rem(z + s, outer), lax.rem(z - s + outer, outer)

    def plane_peer(s):
        return lax.rem(p + s, inner), lax.rem(p - s + inner, inner)

    for w, ref in enumerate((first_ref, second_ref)):
        own = jnp.concatenate(
            [
                ref[...].astype(jnp.float32),
                jnp.zeros((2 * half - rows, channels), jnp.float32),
            ],
            axis=0,
        )
        mine = jnp.where(core == 0, own[:half], own[half:])
        gathered[w, core, me] = mine.astype(jnp.bfloat16)

    barrier = pltpu.get_barrier_semaphore()
    partners = [sibling]
    partners += [(line_peer(s)[0] * inner + p, core) for s in range(1, outer)]
    partners += [(z * inner + plane_peer(s)[0], core) for s in range(1, inner)]
    for device in partners:
        pl.semaphore_signal(barrier, inc=1, device_id=device, device_id_type=MESH)
    pl.semaphore_wait(barrier, len(partners))

    sends = []

    def start(copy):
        copy.start()
        sends.append(copy)

    def line_copy(w, s, source, target):
        place = gathered.at[w, core, source]
        return remote(place, place, line_ws.at[w, s], line_wr.at[w, s], (target, core))

    def plane_copy(w, t, s, source, target):
        place = gathered.at[w, core, source]
        return remote(place, place, plane_ws.at[w, t, s], plane_wr.at[w, t, s], (target, core))

    def core_copy(w, t, which):
        group = pl.ds(line_peer(t)[1] * inner, inner)
        place = gathered.at[w, which, group]
        return remote(place, place, core_ws.at[w, t], core_wr.at[w, t], sibling)

    def send_line(w):
        for s in range(1, outer):
            start(line_copy(w, s, me, line_peer(s)[0] * inner + p))

    def send_plane(w):
        for t in range(outer):
            source = line_peer(t)[1] * inner + p
            if t > 0:
                line_copy(w, t, source, me).wait_recv()
            for s in range(1, inner):
                start(plane_copy(w, t, s, source, z * inner + plane_peer(s)[0]))

    def send_core(w):
        for t in range(outer):
            for s in range(1, inner):
                source = line_peer(t)[1] * inner + plane_peer(s)[1]
                plane_copy(w, t, s, source, me).wait_recv()
            start(core_copy(w, t, core))

    def finish_weight(w):
        for t in range(outer):
            core_copy(w, t, 1 - core).wait_recv()
        for d in range(count):
            base = d * rows
            rows_f32[base : base + half, :] = gathered[w, 0, d].astype(jnp.float32)
            rows_f32[base + half : base + rows, :] = gathered[w, 1, d].astype(jnp.float32)[
                : rows - half
            ]
        for k in range(27):
            block = rows_f32[k * channels : (k + 1) * channels, :].astype(jnp.bfloat16)
            a, rest = divmod(k, 9)
            weights[w, rest * channels : (rest + 1) * channels, a * channels : (a + 1) * channels] = block
            a, rest = divmod(26 - k, 9)
            turned[w, a * channels : (a + 1) * channels, rest * channels : (rest + 1) * channels] = block

    def spread(cols, values):
        field = values.reshape(depth * height, width, channels)
        place = lax.broadcasted_iota(jnp.int32, field.shape, 1)
        left = jnp.where(place == 0, 0.0, pltpu.roll(field, 1, 1))
        right = jnp.where(place == width - 1, 0.0, pltpu.roll(field, width - 1, 1))
        for c, moved in enumerate((left, field, right)):
            moved = moved.reshape(depth, height, width, channels)
            edge = jnp.zeros((depth, 1, width, channels), jnp.float32)
            for b in range(3):
                if b == 0:
                    piece = jnp.concatenate([edge, moved[:, :-1]], axis=1)
                elif b == 1:
                    piece = moved
                else:
                    piece = jnp.concatenate([moved[:, 1:], edge], axis=1)
                k = 3 * b + c
                cols[:, k * channels : (k + 1) * channels] = piece.reshape(cells, channels).astype(
                    jnp.bfloat16
                )

    edge_plane = jnp.zeros((area, channels), jnp.float32)

    def fold_planes(parts):
        before, here, after = (parts[:, a * channels : (a + 1) * channels] for a in range(3))
        return (
            jnp.concatenate([edge_plane, before[:-area]], axis=0)
            + here
            + jnp.concatenate([after[area:], edge_plane], axis=0)
        )

    def forward(cols, w):
        return fold_planes(jnp.dot(cols[...], weights[w], preferred_element_type=jnp.float32))

    def backward(cols, w):
        return fold_planes(
            lax.dot_general(
                cols[...],
                turned[w],
                (((1,), (1,)), ((), ())),
                preferred_element_type=jnp.float32,
            )
        )

    def normalize(values):
        average = jnp.sum(values, axis=0, keepdims=True) / cells
        square_mean = jnp.sum(values * values, axis=0, keepdims=True) / cells
        inverse = lax.rsqrt(square_mean - average * average + EPSILON)
        return (values - average) * inverse, inverse

    def norm_back(grad, normed, inverse):
        plain = jnp.sum(grad, axis=0, keepdims=True) / cells
        paired = jnp.sum(grad * normed, axis=0, keepdims=True) / cells
        return inverse * (grad - plain - normed * paired)

    def weight_grad(cols, delta, g):
        planes[:, :channels] = jnp.concatenate([delta[area:], edge_plane], axis=0).astype(
            jnp.bfloat16
        )
        planes[:, channels : 2 * channels] = delta.astype(jnp.bfloat16)
        planes[:, 2 * channels :] = jnp.concatenate([edge_plane, delta[:-area]], axis=0).astype(
            jnp.bfloat16
        )
        result = lax.dot_general(
            cols[...], planes[...], (((0,), (0,)), ((), ())), preferred_element_type=jnp.float32
        )
        for a in range(3):
            for rest in range(9):
                k = 9 * a + rest
                grad_rows[g, k * channels : (k + 1) * channels, :] = result[
                    rest * channels : (rest + 1) * channels, a * channels : (a + 1) * channels
                ]
        for s in range(1, inner):
            target = plane_peer(s)[0]
            for t in range(outer):
                grad_send[g, s, t] = own_part(g, t * inner + target).astype(jnp.bfloat16)
            start(plane_grad_copy(g, s, z * inner + target))

    def own_part(g, d):
        offset = pl.multiple_of(d * rows + core * half, 8)
        return grad_rows[g, pl.ds(offset, half), :]

    def plane_grad_copy(g, s, target):
        return remote(
            grad_send.at[g, s],
            grad_recv.at[g, s],
            plane_gs.at[g, s],
            plane_gr.at[g, s],
            (target, core),
        )

    def line_grad_copy(g, t, target):
        return remote(
            line_send.at[g, t],
            line_recv.at[g, t],
            line_gs.at[g, t],
            line_gr.at[g, t],
            (target, core),
        )

    def core_grad_copy(g, which):
        place = halves.at[g, which]
        return remote(place, place, core_gs.at[g], core_gr.at[g], sibling)

    def reduce_plane(g):
        for s in range(1, inner):
            plane_grad_copy(g, s, me).wait_recv()
        for t in range(1, outer):
            target = line_peer(t)[0]
            total = own_part(g, target * inner + p)
            for s in range(1, inner):
                total = total + grad_recv[g, s, target].astype(jnp.float32)
            line_send[g, t] = total.astype(jnp.bfloat16)
            start(line_grad_copy(g, t, target * inner + p))
        total = own_part(g, me)
        for s in range(1, inner):
            total = total + grad_recv[g, s, z].astype(jnp.float32)
        halves[g, core] = total

    def reduce_line(g):
        total = halves[g, core]
        for t in range(1, outer):
            line_grad_copy(g, t, me).wait_recv()
            total = total + line_recv[g, t].astype(jnp.float32)
        halves[g, core] = total * factor
        start(core_grad_copy(g, core))

    def write_grad(g, ref):
        core_grad_copy(g, 1 - core).wait_recv()
        ref[0:half, :] = halves[g, 0]
        ref[half:rows, :] = halves[g, 1][: rows - half]

    send_line(0)
    own_rows = pl.ds(pl.multiple_of(core * own_cells, own_cells), own_cells)
    other_rows = pl.ds(pl.multiple_of((1 - core) * own_cells, own_cells), own_cells)
    for f, ref in enumerate((image_ref, cotangent_ref)):
        start(
            remote(ref, fields.at[f, own_rows], field_send.at[f], field_recv.at[f], sibling)
        )
        fields[f, own_rows, :] = ref[...]
    send_line(1)
    grad_rows[:, count * rows :, :] = jnp.zeros_like(grad_rows[:, count * rows :, :])
    send_plane(0)
    for f, ref in enumerate((image_ref, cotangent_ref)):
        remote(
            ref, fields.at[f, other_rows], field_send.at[f], field_recv.at[f], sibling
        ).wait_recv()
    spread(image_cols, fields[0].astype(jnp.float32))
    send_core(0)
    send_plane(1)
    finish_weight(0)

    first_norm, first_inverse = normalize(forward(image_cols, 0))
    hidden = gelu_value(first_norm).astype(jnp.bfloat16)
    spread(hidden_cols, hidden.astype(jnp.float32))
    send_core(1)
    finish_weight(1)
    second_norm, second_inverse = normalize(forward(hidden_cols, 1))
    summed = fields[0].astype(jnp.float32) + second_norm
    summed_ref[...] = summed
    outer_grad = fields[1].astype(jnp.float32) * gelu_slope(summed)
    outer_ref[...] = outer_grad
    second_delta = norm_back(outer_grad, second_norm, second_inverse)
    second_delta = second_delta.astype(jnp.bfloat16).astype(jnp.float32)
    weight_grad(hidden_cols, second_delta, 1)
    spread(delta_cols, second_delta)
    inner_grad = backward(delta_cols, 1)
    first_delta = norm_back(inner_grad * gelu_slope(first_norm), first_norm, first_inverse)
    first_delta = first_delta.astype(jnp.bfloat16).astype(jnp.float32)
    weight_grad(image_cols, first_delta, 0)
    reduce_plane(1)
    spread(delta_cols, first_delta)
    outer_ref[...] = outer_ref[...] + backward(delta_cols, 0)
    image_grad_ref[...] = outer_ref[own_rows, :].astype(jnp.bfloat16)
    output_ref[...] = gelu_value(summed_ref[own_rows, :]).astype(jnp.bfloat16)
    reduce_line(1)
    reduce_plane(0)
    write_grad(1, second_grad_ref)
    reduce_line(0)
    write_grad(0, first_grad_ref)
    for copy in sends:
        copy.wait_send()


def fused(count, image, cotangent, first_weight, second_weight):
    _, depth, height, width, channels = image.shape
    own_cells = depth * height * width
    cells = 2 * own_cells
    rows = first_weight.shape[0]
    half = -(-rows // 32) * 16
    inner = group_size(count)
    outer = count // inner
    sizes = (count, inner, 2 * depth, height, width, channels, rows)
    bf16, f32 = jnp.bfloat16, jnp.float32
    dma = pltpu.SemaphoreType.DMA
    whole = pl.BlockSpec(memory_space=pltpu.VMEM)
    output, image_grad, first_grad, second_grad = pl.pallas_call(
        functools.partial(block_kernel, sizes),
        out_shape=(
            jax.ShapeDtypeStruct((own_cells, channels), bf16),
            jax.ShapeDtypeStruct((own_cells, channels), bf16),
            jax.ShapeDtypeStruct((rows, channels), f32),
            jax.ShapeDtypeStruct((rows, channels), f32),
        ),
        in_specs=[whole] * 4,
        out_specs=(whole,) * 4,
        scratch_shapes=[
            pltpu.VMEM((2, cells, channels), bf16),
            pltpu.VMEM((2, 2, count, half, channels), bf16),
            pltpu.VMEM((27 * channels, channels), f32),
            pltpu.VMEM((2, 9 * channels, 3 * channels), bf16),
            pltpu.VMEM((2, 3 * channels, 9 * channels), bf16),
            pltpu.VMEM((cells, 9 * channels), bf16),
            pltpu.VMEM((cells, 9 * channels), bf16),
            pltpu.VMEM((cells, 9 * channels), bf16),
            pltpu.VMEM((cells, 3 * channels), bf16),
            pltpu.VMEM((2, 27 * channels + 2 * half - rows, channels), f32),
            pltpu.VMEM((2, inner, outer, half, channels), bf16),
            pltpu.VMEM((2, inner, outer, half, channels), bf16),
            pltpu.VMEM((2, outer, half, channels), bf16),
            pltpu.VMEM((2, outer, half, channels), bf16),
            pltpu.VMEM((2, 2, half, channels), f32),
            pltpu.VMEM((cells, channels), f32),
            pltpu.VMEM((cells, channels), f32),
            dma((2,)),
            dma((2,)),
            dma((2, outer)),
            dma((2, outer)),
            dma((2, outer, inner)),
            dma((2, outer, inner)),
            dma((2, outer)),
            dma((2, outer)),
            dma((2, inner)),
            dma((2, inner)),
            dma((2, outer)),
            dma((2, outer)),
            dma((2,)),
            dma((2,)),
        ],
        compiler_params=pltpu.CompilerParams(
            collective_id=0, has_side_effects=True, vmem_limit_bytes=56 * 1024 * 1024
        ),
        cost_estimate=pl.CostEstimate(
            flops=12 * cells * 27 * channels * channels,
            bytes_accessed=12 * own_cells * channels,
            transcendentals=6 * cells * channels,
        ),
    )(
        image.reshape(own_cells, channels),
        cotangent.reshape(own_cells, channels),
        first_weight,
        second_weight,
    )
    return output.reshape(image.shape), image_grad.reshape(image.shape), first_grad, second_grad


def fits_kernel(count, slabs, image, first_weight):
    _, depth, height, width, channels = image.shape
    rows = first_weight.shape[0]
    inner = group_size(count)
    return (
        slabs == 2
        and image.shape[0] == 1
        and inner > 1
        and count // inner > 1
        and width % 8 == 0
        and channels % 128 == 0
        and rows % 8 == 0
        and depth * height * width <= 512
    )


def block(image, cotangent, first_weight, second_weight):
    count, slabs = lax.axis_size("dp"), lax.axis_size("space")
    if fits_kernel(count, slabs, image, first_weight):
        return fused(count, image, cotangent, first_weight, second_weight)
    return local(image, cotangent, first_weight, second_weight)


def solution(mesh):
    return jax.shard_map(
        block,
        mesh=mesh,
        in_specs=(
            P("dp", "space", None, None, None),
            P("dp", "space", None, None, None),
            P("dp", None),
            P("dp", None),
        ),
        out_specs=(
            P("dp", "space", None, None, None),
            P("dp", "space", None, None, None),
            P("dp", None),
            P("dp", None),
        ),
        check_vma=False,
    )
```

```python
import functools
import math

import jax
import jax.numpy as jnp
from jax import lax
from jax.experimental import pallas as pl
from jax.experimental.pallas import tpu as pltpu
from jax.sharding import PartitionSpec as P

MESH = pl.DeviceIdType.MESH

EPSILON = 1e-05


def with_halo(cells, sides, width):
    for axis, dim in sides:
        count = lax.axis_size(axis)
        ends = count - 1
        head = lax.slice_in_dim(cells, 0, width, axis=dim)
        tail = lax.slice_in_dim(cells, cells.shape[dim] - width, cells.shape[dim], axis=dim)
        cells = jnp.concatenate(
            [
                lax.ppermute(tail, axis, [(i, (i + 1) % count) for i in range(ends)]),
                cells,
                lax.ppermute(head, axis, [((i + 1) % count, i) for i in range(ends)]),
            ],
            axis=dim,
        )
    return cells


def gelu_value(values):
    return 0.5 * values * (1.0 + lax.erf(values * 0.7071067811865476))


def gelu_slope(values):
    return (
        0.5 * (1.0 + lax.erf(values * 0.7071067811865476))
        + values * jnp.exp(-0.5 * values * values) * 0.3989422804014327
    )


def columns(deep):
    depth = deep.shape[0] - 2
    height, width, channels = (deep.shape[1], deep.shape[2], deep.shape[3])
    padded = jnp.pad(deep, ((0, 0), (1, 1), (1, 1), (0, 0)))
    pieces = [
        padded[first : first + depth, second : second + height, third : third + width, :]
        for first in range(3)
        for second in range(3)
        for third in range(3)
    ]
    return jnp.concatenate(pieces, axis=-1).reshape(depth * height * width, 27 * channels)


def reverse_taps(weight):
    channels = weight.shape[1]
    return (
        weight.reshape(27, channels, channels)[::-1]
        .transpose(0, 2, 1)
        .reshape(27 * channels, channels)
    )


def local(image, cotangent, first_weight, second_weight):
    slab = image[0]
    depth, height, width, channels = slab.shape
    cells = depth * height * width
    patch_cells = cells * lax.axis_size("space")
    factor = 1.0 / math.sqrt(patch_cells * lax.axis_size("dp"))

    def unfold_slab(volume):
        deep = with_halo(volume, (("space", 0),), 1)
        return columns(deep)

    def normalize(values):
        totals, squares = lax.psum(
            (jnp.sum(values, axis=0), jnp.sum(values * values, axis=0)), "space"
        )
        average = totals / patch_cells
        inverse = lax.rsqrt(squares / patch_cells - average * average + EPSILON)
        return ((values - average) * inverse, inverse)

    def norm_back(grad, normed, inverse):
        plain_total, paired_total = lax.psum(
            (jnp.sum(grad, axis=0), jnp.sum(grad * normed, axis=0)), "space"
        )
        return inverse * (grad - plain_total / patch_cells - normed * (paired_total / patch_cells))

    def apply_weight(unfolded, shard):
        whole = lax.all_gather(shard, "dp", axis=0, tiled=True)
        return (jnp.dot(unfolded, whole, preferred_element_type=jnp.float32), shard)

    def weight_again(kept):
        whole = lax.all_gather(kept, "dp", axis=0, tiled=True)
        return reverse_taps(whole)

    def reduce_grad(unfolded, delta):
        own_rows = lax.psum_scatter(
            lax.dot_general(
                unfolded, delta, (((0,), (0,)), ((), ())), preferred_element_type=jnp.float32
            ),
            "dp",
            scatter_dimension=0,
            tiled=True,
        )
        return lax.psum(own_rows, "space")

    first_columns = unfold_slab(slab)
    first_conv, first_kept = apply_weight(first_columns, first_weight)
    first_norm, first_inverse = normalize(first_conv)
    hidden = gelu_value(first_norm).astype(jnp.bfloat16)
    second_columns = unfold_slab(hidden.reshape(depth, height, width, channels))
    second_conv, second_kept = apply_weight(second_columns, second_weight)
    second_norm, second_inverse = normalize(second_conv)
    summed = slab.reshape(cells, channels).astype(jnp.float32) + second_norm
    output = gelu_value(summed).astype(jnp.bfloat16)
    outer_grad = cotangent[0].reshape(cells, channels).astype(jnp.float32) * gelu_slope(summed)
    second_delta = norm_back(outer_grad, second_norm, second_inverse).astype(jnp.bfloat16)
    second_grad = reduce_grad(second_columns, second_delta)
    inner_grad = jnp.dot(
        unfold_slab(second_delta.reshape(depth, height, width, channels)),
        weight_again(second_kept),
        preferred_element_type=jnp.float32,
    )
    first_delta = norm_back(inner_grad * gelu_slope(first_norm), first_norm, first_inverse).astype(
        jnp.bfloat16
    )
    first_grad = reduce_grad(first_columns, first_delta)
    backward_term = jnp.dot(
        unfold_slab(first_delta.reshape(depth, height, width, channels)),
        weight_again(first_kept),
        preferred_element_type=jnp.float32,
    )
    image_grad = (outer_grad + backward_term).astype(jnp.bfloat16)
    return (
        output.reshape(image.shape),
        image_grad.reshape(image.shape),
        first_grad * factor,
        second_grad * factor,
    )


def group_size(count):
    size = 1
    while size * size < count and count % (2 * size) == 0:
        size *= 2
    return size


def remote(src, dst, send_sem, recv_sem, device):
    return pltpu.make_async_remote_copy(
        src_ref=src,
        dst_ref=dst,
        send_sem=send_sem,
        recv_sem=recv_sem,
        device_id=device,
        device_id_type=MESH,
    )


def block_kernel(
    sizes,
    image_ref,
    cotangent_ref,
    first_ref,
    second_ref,
    output_ref,
    image_grad_ref,
    first_grad_ref,
    second_grad_ref,
    fields,
    gathered,
    rows_f32,
    weights,
    turned,
    image_cols,
    hidden_cols,
    delta_cols,
    planes,
    grad_rows,
    grad_send,
    grad_recv,
    line_send,
    line_recv,
    halves,
    summed_ref,
    outer_ref,
    field_send,
    field_recv,
    line_ws,
    line_wr,
    plane_ws,
    plane_wr,
    core_ws,
    core_wr,
    plane_gs,
    plane_gr,
    line_gs,
    line_gr,
    core_gs,
    core_gr,
):
    count, inner, depth, height, width, channels, rows = sizes
    outer = count // inner
    half = gathered.shape[3]
    cells = depth * height * width
    own_cells = cells // 2
    area = height * width
    factor = 1.0 / math.sqrt(cells * count)
    me = lax.axis_index("dp")
    core = lax.axis_index("space")
    z = lax.div(me, inner)
    p = lax.rem(me, inner)
    sibling = (me, 1 - core)

    def flipped(value, mask):
        bit = 1
        while bit <= mask:
            if mask & bit:
                value = value + bit - 2 * bit * lax.rem(lax.div(value, bit), 2)
            bit *= 2
        return value

    def line_peer(s):
        return flipped(z, s)

    def plane_peer(s):
        return flipped(p, s)

    barrier = pltpu.get_barrier_semaphore()
    partners = [sibling]
    partners += [(line_peer(s) * inner + p, core) for s in range(1, outer)]
    partners += [(z * inner + plane_peer(s), core) for s in range(1, inner)]
    for device in partners:
        pl.semaphore_signal(barrier, inc=1, device_id=device, device_id_type=MESH)
    for w, ref in enumerate((first_ref, second_ref)):
        own = jnp.concatenate(
            [
                ref[...].astype(jnp.float32),
                jnp.zeros((2 * half - rows, channels), jnp.float32),
            ],
            axis=0,
        )
        mine = jnp.where(core == 0, own[:half], own[half:])
        gathered[w, core, me] = mine.astype(jnp.bfloat16)

    pl.semaphore_wait(barrier, len(partners))

    sends = []

    def start(copy):
        copy.start()
        sends.append(copy)

    def line_copy(w, s, source, target):
        place = gathered.at[w, core, source]
        return remote(place, place, line_ws.at[w, s], line_wr.at[w, s], (target, core))

    def plane_copy(w, t, s, source, target):
        place = gathered.at[w, core, source]
        return remote(place, place, plane_ws.at[w, t, s], plane_wr.at[w, t, s], (target, core))

    def core_copy(w, t, which):
        group = pl.ds(line_peer(t) * inner, inner)
        place = gathered.at[w, which, group]
        return remote(place, place, core_ws.at[w, t], core_wr.at[w, t], sibling)

    def send_line(w):
        for s in range(1, outer):
            start(line_copy(w, s, me, line_peer(s) * inner + p))

    def send_plane(w, t):
        source = line_peer(t) * inner + p
        if t > 0:
            line_copy(w, t, source, me).wait_recv()
        for s in range(1, inner):
            start(plane_copy(w, t, s, source, z * inner + plane_peer(s)))

    def send_core(w):
        for t in range(outer):
            for s in range(1, inner):
                source = line_peer(t) * inner + plane_peer(s)
                plane_copy(w, t, s, source, me).wait_recv()
            start(core_copy(w, t, core))

    def finish_weight(w):
        for t in range(outer):
            core_copy(w, t, 1 - core).wait_recv()
        for d in range(count):
            base = d * rows
            rows_f32[base : base + half, :] = gathered[w, 0, d].astype(jnp.float32)
            rows_f32[base + half : base + rows, :] = gathered[w, 1, d].astype(jnp.float32)[
                : rows - half
            ]
        for k in range(27):
            block = rows_f32[k * channels : (k + 1) * channels, :].astype(jnp.bfloat16)
            a, rest = divmod(k, 9)
            weights[w, rest * channels : (rest + 1) * channels, a * channels : (a + 1) * channels] = block
            a, rest = divmod(26 - k, 9)
            turned[w, a * channels : (a + 1) * channels, rest * channels : (rest + 1) * channels] = block

    def spread(cols, values):
        field = values.reshape(depth * height, width, channels)
        place = lax.broadcasted_iota(jnp.int32, field.shape, 1)
        left = jnp.where(place == 0, 0.0, pltpu.roll(field, 1, 1))
        right = jnp.where(place == width - 1, 0.0, pltpu.roll(field, width - 1, 1))
        for c, moved in enumerate((left, field, right)):
            moved = moved.reshape(depth, height, width, channels)
            edge = jnp.zeros((depth, 1, width, channels), jnp.float32)
            for b in range(3):
                if b == 0:
                    piece = jnp.concatenate([edge, moved[:, :-1]], axis=1)
                elif b == 1:
                    piece = moved
                else:
                    piece = jnp.concatenate([moved[:, 1:], edge], axis=1)
                k = 3 * b + c
                cols[:, k * channels : (k + 1) * channels] = piece.reshape(cells, channels).astype(
                    jnp.bfloat16
                )

    edge_plane = jnp.zeros((area, channels), jnp.float32)

    def fold_planes(parts):
        before, here, after = (parts[:, a * channels : (a + 1) * channels] for a in range(3))
        return (
            jnp.concatenate([edge_plane, before[:-area]], axis=0)
            + here
            + jnp.concatenate([after[area:], edge_plane], axis=0)
        )

    def forward(cols, w):
        return fold_planes(jnp.dot(cols[...], weights[w], preferred_element_type=jnp.float32))

    def backward(cols, w):
        return fold_planes(
            lax.dot_general(
                cols[...],
                turned[w],
                (((1,), (1,)), ((), ())),
                preferred_element_type=jnp.float32,
            )
        )

    def normalize(values):
        average = jnp.sum(values, axis=0, keepdims=True) / cells
        square_mean = jnp.sum(values * values, axis=0, keepdims=True) / cells
        inverse = lax.rsqrt(square_mean - average * average + EPSILON)
        return (values - average) * inverse, inverse

    def norm_back(grad, normed, inverse):
        plain = jnp.sum(grad, axis=0, keepdims=True) / cells
        paired = jnp.sum(grad * normed, axis=0, keepdims=True) / cells
        return inverse * (grad - plain - normed * paired)

    def weight_grad(cols, delta, g):
        planes[:, :channels] = jnp.concatenate([delta[area:], edge_plane], axis=0).astype(
            jnp.bfloat16
        )
        planes[:, channels : 2 * channels] = delta.astype(jnp.bfloat16)
        planes[:, 2 * channels :] = jnp.concatenate([edge_plane, delta[:-area]], axis=0).astype(
            jnp.bfloat16
        )
        result = lax.dot_general(
            cols[...], planes[...], (((0,), (0,)), ((), ())), preferred_element_type=jnp.float32
        )
        for a in range(3):
            for rest in range(9):
                k = 9 * a + rest
                grad_rows[g, k * channels : (k + 1) * channels, :] = result[
                    rest * channels : (rest + 1) * channels, a * channels : (a + 1) * channels
                ]
        for t in reversed(range(outer)):
            for s in range(1, inner):
                target = plane_peer(s)
                part = own_part(g, line_peer(t) * inner + target)
                grad_send[g, s, t] = part.astype(jnp.bfloat16)
                start(plane_grad_copy(g, s, t, z * inner + target))

    def own_part(g, d):
        offset = pl.multiple_of(d * rows + core * half, 8)
        return grad_rows[g, pl.ds(offset, half), :]

    def plane_grad_copy(g, s, t, target):
        return remote(
            grad_send.at[g, s, t],
            grad_recv.at[g, s, t],
            plane_gs.at[g, s, t],
            plane_gr.at[g, s, t],
            (target, core),
        )

    def line_grad_copy(g, t, target):
        return remote(
            line_send.at[g, t],
            line_recv.at[g, t],
            line_gs.at[g, t],
            line_gr.at[g, t],
            (target, core),
        )

    def core_grad_copy(g, which):
        place = halves.at[g, which]
        return remote(place, place, core_gs.at[g], core_gr.at[g], sibling)

    def reduce_plane(g):
        for t in reversed(range(outer)):
            target = line_peer(t) * inner + p
            total = own_part(g, target)
            for s in range(1, inner):
                plane_grad_copy(g, s, t, me).wait_recv()
                total = total + grad_recv[g, s, t].astype(jnp.float32)
            if t > 0:
                line_send[g, t] = total.astype(jnp.bfloat16)
                start(line_grad_copy(g, t, target))
            else:
                halves[g, core] = total

    def reduce_line(g):
        total = halves[g, core]
        for t in range(1, outer):
            line_grad_copy(g, t, me).wait_recv()
            total = total + line_recv[g, t].astype(jnp.float32)
        halves[g, core] = total * factor
        start(core_grad_copy(g, core))

    def write_grad(g, ref):
        core_grad_copy(g, 1 - core).wait_recv()
        ref[0:half, :] = halves[g, 0]
        ref[half:rows, :] = halves[g, 1][: rows - half]

    send_line(0)
    send_plane(0, 0)
    send_plane(1, 0)
    own_rows = pl.ds(pl.multiple_of(core * own_cells, own_cells), own_cells)
    other_rows = pl.ds(pl.multiple_of((1 - core) * own_cells, own_cells), own_cells)
    for f, ref in enumerate((image_ref, cotangent_ref)):
        start(
            remote(ref, fields.at[f, own_rows], field_send.at[f], field_recv.at[f], sibling)
        )
        fields[f, own_rows, :] = ref[...]
    send_plane(0, 1)
    send_line(1)
    for t in range(2, outer):
        send_plane(0, t)
    grad_rows[:, count * rows :, :] = jnp.zeros_like(grad_rows[:, count * rows :, :])
    for f, ref in enumerate((image_ref, cotangent_ref)):
        remote(
            ref, fields.at[f, other_rows], field_send.at[f], field_recv.at[f], sibling
        ).wait_recv()
    spread(image_cols, fields[0].astype(jnp.float32))
    for t in range(1, outer):
        send_plane(1, t)
    send_core(0)
    finish_weight(0)

    first_norm, first_inverse = normalize(forward(image_cols, 0))
    hidden = gelu_value(first_norm).astype(jnp.bfloat16)
    spread(hidden_cols, hidden.astype(jnp.float32))
    send_core(1)
    finish_weight(1)
    second_norm, second_inverse = normalize(forward(hidden_cols, 1))
    summed = fields[0].astype(jnp.float32) + second_norm
    summed_ref[...] = summed
    outer_grad = fields[1].astype(jnp.float32) * gelu_slope(summed)
    outer_ref[...] = outer_grad
    second_delta = norm_back(outer_grad, second_norm, second_inverse)
    second_delta = second_delta.astype(jnp.bfloat16).astype(jnp.float32)
    weight_grad(hidden_cols, second_delta, 1)
    spread(delta_cols, second_delta)
    inner_grad = backward(delta_cols, 1)
    first_delta = norm_back(inner_grad * gelu_slope(first_norm), first_norm, first_inverse)
    first_delta = first_delta.astype(jnp.bfloat16).astype(jnp.float32)
    weight_grad(image_cols, first_delta, 0)
    spread(delta_cols, first_delta)
    outer_ref[...] = outer_ref[...] + backward(delta_cols, 0)
    image_grad_ref[...] = outer_ref[own_rows, :].astype(jnp.bfloat16)
    output_ref[...] = gelu_value(summed_ref[own_rows, :]).astype(jnp.bfloat16)
    reduce_plane(1)
    reduce_plane(0)
    reduce_line(1)
    write_grad(1, second_grad_ref)
    reduce_line(0)
    write_grad(0, first_grad_ref)
    for copy in sends:
        copy.wait_send()


def hand_over(*results):
    def kernel(*refs):
        for source, target in zip(refs[: len(results)], refs[len(results) :]):
            target[...] = source[...]

    whole = pl.BlockSpec(memory_space=pltpu.VMEM)
    return pl.pallas_call(
        kernel,
        out_shape=tuple(jax.ShapeDtypeStruct(x.shape, x.dtype) for x in results),
        in_specs=[whole] * len(results),
        out_specs=(whole,) * len(results),
    )(*results)


def fused(count, image, cotangent, first_weight, second_weight):
    _, depth, height, width, channels = image.shape
    own_cells = depth * height * width
    cells = 2 * own_cells
    rows = first_weight.shape[0]
    half = -(-rows // 32) * 16
    inner = group_size(count)
    outer = count // inner
    sizes = (count, inner, 2 * depth, height, width, channels, rows)
    bf16, f32 = jnp.bfloat16, jnp.float32
    dma = pltpu.SemaphoreType.DMA
    whole = pl.BlockSpec(memory_space=pltpu.VMEM)
    output, image_grad, first_grad, second_grad = pl.pallas_call(
        functools.partial(block_kernel, sizes),
        out_shape=(
            jax.ShapeDtypeStruct((own_cells, channels), bf16),
            jax.ShapeDtypeStruct((own_cells, channels), bf16),
            jax.ShapeDtypeStruct((rows, channels), f32),
            jax.ShapeDtypeStruct((rows, channels), f32),
        ),
        in_specs=[whole] * 4,
        out_specs=(whole,) * 4,
        scratch_shapes=[
            pltpu.VMEM((2, cells, channels), bf16),
            pltpu.VMEM((2, 2, count, half, channels), bf16),
            pltpu.VMEM((27 * channels, channels), f32),
            pltpu.VMEM((2, 9 * channels, 3 * channels), bf16),
            pltpu.VMEM((2, 3 * channels, 9 * channels), bf16),
            pltpu.VMEM((cells, 9 * channels), bf16),
            pltpu.VMEM((cells, 9 * channels), bf16),
            pltpu.VMEM((cells, 9 * channels), bf16),
            pltpu.VMEM((cells, 3 * channels), bf16),
            pltpu.VMEM((2, 27 * channels + 2 * half - rows, channels), f32),
            pltpu.VMEM((2, inner, outer, half, channels), bf16),
            pltpu.VMEM((2, inner, outer, half, channels), bf16),
            pltpu.VMEM((2, outer, half, channels), bf16),
            pltpu.VMEM((2, outer, half, channels), bf16),
            pltpu.VMEM((2, 2, half, channels), f32),
            pltpu.VMEM((cells, channels), f32),
            pltpu.VMEM((cells, channels), f32),
            dma((2,)),
            dma((2,)),
            dma((2, outer)),
            dma((2, outer)),
            dma((2, outer, inner)),
            dma((2, outer, inner)),
            dma((2, outer)),
            dma((2, outer)),
            dma((2, inner, outer)),
            dma((2, inner, outer)),
            dma((2, outer)),
            dma((2, outer)),
            dma((2,)),
            dma((2,)),
        ],
        compiler_params=pltpu.CompilerParams(
            collective_id=0, has_side_effects=True, vmem_limit_bytes=56 * 1024 * 1024
        ),
        cost_estimate=pl.CostEstimate(
            flops=12 * cells * 27 * channels * channels,
            bytes_accessed=12 * own_cells * channels,
            transcendentals=6 * cells * channels,
        ),
    )(
        image.reshape(own_cells, channels),
        cotangent.reshape(own_cells, channels),
        first_weight,
        second_weight,
    )
    output, image_grad, first_grad, second_grad = hand_over(
        output, image_grad, first_grad, second_grad
    )
    return output.reshape(image.shape), image_grad.reshape(image.shape), first_grad, second_grad


def fits_kernel(count, slabs, image, first_weight):
    _, depth, height, width, channels = image.shape
    rows = first_weight.shape[0]
    inner = group_size(count)
    return (
        slabs == 2
        and image.shape[0] == 1
        and inner > 1
        and count // inner > 1
        and (count & (count - 1)) == 0
        and width % 8 == 0
        and channels % 128 == 0
        and rows % 8 == 0
        and depth * height * width <= 512
    )


def block(image, cotangent, first_weight, second_weight):
    count, slabs = lax.axis_size("dp"), lax.axis_size("space")
    if fits_kernel(count, slabs, image, first_weight):
        return fused(count, image, cotangent, first_weight, second_weight)
    return local(image, cotangent, first_weight, second_weight)


def solution(mesh):
    return jax.shard_map(
        block,
        mesh=mesh,
        in_specs=(
            P("dp", "space", None, None, None),
            P("dp", "space", None, None, None),
            P("dp", None),
            P("dp", None),
        ),
        out_specs=(
            P("dp", "space", None, None, None),
            P("dp", "space", None, None, None),
            P("dp", None),
            P("dp", None),
        ),
        check_vma=False,
    )
```

```python
import functools
import math

import jax
import jax.numpy as jnp
from jax import lax
from jax.experimental import pallas as pl
from jax.experimental.pallas import tpu as pltpu
from jax.sharding import PartitionSpec as P

MESH = pl.DeviceIdType.MESH

EPSILON = 1e-05


def with_halo(cells, sides, width):
    for axis, dim in sides:
        count = lax.axis_size(axis)
        ends = count - 1
        head = lax.slice_in_dim(cells, 0, width, axis=dim)
        tail = lax.slice_in_dim(cells, cells.shape[dim] - width, cells.shape[dim], axis=dim)
        cells = jnp.concatenate(
            [
                lax.ppermute(tail, axis, [(i, (i + 1) % count) for i in range(ends)]),
                cells,
                lax.ppermute(head, axis, [((i + 1) % count, i) for i in range(ends)]),
            ],
            axis=dim,
        )
    return cells


def gelu_value(values):
    return 0.5 * values * (1.0 + lax.erf(values * 0.7071067811865476))


def gelu_slope(values):
    return (
        0.5 * (1.0 + lax.erf(values * 0.7071067811865476))
        + values * jnp.exp(-0.5 * values * values) * 0.3989422804014327
    )


def columns(deep):
    depth = deep.shape[0] - 2
    height, width, channels = (deep.shape[1], deep.shape[2], deep.shape[3])
    padded = jnp.pad(deep, ((0, 0), (1, 1), (1, 1), (0, 0)))
    pieces = [
        padded[first : first + depth, second : second + height, third : third + width, :]
        for first in range(3)
        for second in range(3)
        for third in range(3)
    ]
    return jnp.concatenate(pieces, axis=-1).reshape(depth * height * width, 27 * channels)


def reverse_taps(weight):
    channels = weight.shape[1]
    return (
        weight.reshape(27, channels, channels)[::-1]
        .transpose(0, 2, 1)
        .reshape(27 * channels, channels)
    )


def local(image, cotangent, first_weight, second_weight):
    slab = image[0]
    depth, height, width, channels = slab.shape
    cells = depth * height * width
    patch_cells = cells * lax.axis_size("space")
    factor = 1.0 / math.sqrt(patch_cells * lax.axis_size("dp"))

    def unfold_slab(volume):
        deep = with_halo(volume, (("space", 0),), 1)
        return columns(deep)

    def normalize(values):
        totals, squares = lax.psum(
            (jnp.sum(values, axis=0), jnp.sum(values * values, axis=0)), "space"
        )
        average = totals / patch_cells
        inverse = lax.rsqrt(squares / patch_cells - average * average + EPSILON)
        return ((values - average) * inverse, inverse)

    def norm_back(grad, normed, inverse):
        plain_total, paired_total = lax.psum(
            (jnp.sum(grad, axis=0), jnp.sum(grad * normed, axis=0)), "space"
        )
        return inverse * (grad - plain_total / patch_cells - normed * (paired_total / patch_cells))

    def apply_weight(unfolded, shard):
        whole = lax.all_gather(shard, "dp", axis=0, tiled=True)
        return (jnp.dot(unfolded, whole, preferred_element_type=jnp.float32), shard)

    def weight_again(kept):
        whole = lax.all_gather(kept, "dp", axis=0, tiled=True)
        return reverse_taps(whole)

    def reduce_grad(unfolded, delta):
        own_rows = lax.psum_scatter(
            lax.dot_general(
                unfolded, delta, (((0,), (0,)), ((), ())), preferred_element_type=jnp.float32
            ),
            "dp",
            scatter_dimension=0,
            tiled=True,
        )
        return lax.psum(own_rows, "space")

    first_columns = unfold_slab(slab)
    first_conv, first_kept = apply_weight(first_columns, first_weight)
    first_norm, first_inverse = normalize(first_conv)
    hidden = gelu_value(first_norm).astype(jnp.bfloat16)
    second_columns = unfold_slab(hidden.reshape(depth, height, width, channels))
    second_conv, second_kept = apply_weight(second_columns, second_weight)
    second_norm, second_inverse = normalize(second_conv)
    summed = slab.reshape(cells, channels).astype(jnp.float32) + second_norm
    output = gelu_value(summed).astype(jnp.bfloat16)
    outer_grad = cotangent[0].reshape(cells, channels).astype(jnp.float32) * gelu_slope(summed)
    second_delta = norm_back(outer_grad, second_norm, second_inverse).astype(jnp.bfloat16)
    second_grad = reduce_grad(second_columns, second_delta)
    inner_grad = jnp.dot(
        unfold_slab(second_delta.reshape(depth, height, width, channels)),
        weight_again(second_kept),
        preferred_element_type=jnp.float32,
    )
    first_delta = norm_back(inner_grad * gelu_slope(first_norm), first_norm, first_inverse).astype(
        jnp.bfloat16
    )
    first_grad = reduce_grad(first_columns, first_delta)
    backward_term = jnp.dot(
        unfold_slab(first_delta.reshape(depth, height, width, channels)),
        weight_again(first_kept),
        preferred_element_type=jnp.float32,
    )
    image_grad = (outer_grad + backward_term).astype(jnp.bfloat16)
    return (
        output.reshape(image.shape),
        image_grad.reshape(image.shape),
        first_grad * factor,
        second_grad * factor,
    )


def group_size(count):
    size = 1
    while size * size < count and count % (2 * size) == 0:
        size *= 2
    return size


def remote(src, dst, send_sem, recv_sem, device):
    return pltpu.make_async_remote_copy(
        src_ref=src,
        dst_ref=dst,
        send_sem=send_sem,
        recv_sem=recv_sem,
        device_id=device,
        device_id_type=MESH,
    )


def block_kernel(
    sizes,
    image_ref,
    cotangent_ref,
    first_ref,
    second_ref,
    output_ref,
    image_grad_ref,
    first_grad_ref,
    second_grad_ref,
    fields,
    gathered,
    rows_f32,
    weights,
    turned,
    image_cols,
    hidden_cols,
    delta_cols,
    planes,
    grad_rows,
    grad_send,
    grad_recv,
    near_send,
    near_recv,
    line_send,
    line_recv,
    halves,
    summed_ref,
    outer_ref,
    field_send,
    field_recv,
    line_ws,
    line_wr,
    plane_ws,
    plane_wr,
    core_ws,
    core_wr,
    plane_gs,
    plane_gr,
    near_gs,
    near_gr,
    line_gs,
    line_gr,
    core_gs,
    core_gr,
):
    count, inner, depth, height, width, channels, rows = sizes
    outer = count // inner
    half = gathered.shape[3]
    cells = depth * height * width
    own_cells = cells // 2
    area = height * width
    factor = 1.0 / math.sqrt(cells * count)
    me = lax.axis_index("dp")
    core = lax.axis_index("space")
    z = lax.div(me, inner)
    p = lax.rem(me, inner)
    sibling = (me, 1 - core)

    def flipped(value, mask):
        bit = 1
        while bit <= mask:
            if mask & bit:
                value = value + bit - 2 * bit * lax.rem(lax.div(value, bit), 2)
            bit *= 2
        return value

    def line_peer(s):
        return flipped(z, s)

    def plane_peer(s):
        return flipped(p, s)

    barrier = pltpu.get_barrier_semaphore()
    partners = [sibling]
    partners += [(line_peer(s) * inner + p, core) for s in range(1, outer)]
    partners += [(z * inner + plane_peer(s), core) for s in range(1, inner)]
    for device in partners:
        pl.semaphore_signal(barrier, inc=1, device_id=device, device_id_type=MESH)
    for w, ref in enumerate((first_ref, second_ref)):
        own = jnp.concatenate(
            [
                ref[...].astype(jnp.float32),
                jnp.zeros((2 * half - rows, channels), jnp.float32),
            ],
            axis=0,
        )
        mine = jnp.where(core == 0, own[:half], own[half:])
        gathered[w, core, me] = mine.astype(jnp.bfloat16)

    pl.semaphore_wait(barrier, len(partners))

    sends = []

    def start(copy):
        copy.start()
        sends.append(copy)

    def line_copy(w, s, source, target):
        place = gathered.at[w, core, source]
        return remote(place, place, line_ws.at[w, s], line_wr.at[w, s], (target, core))

    def plane_copy(w, t, s, source, target):
        place = gathered.at[w, core, source]
        return remote(place, place, plane_ws.at[w, t, s], plane_wr.at[w, t, s], (target, core))

    def core_copy(w, t, which):
        group = pl.ds(line_peer(t) * inner, inner)
        place = gathered.at[w, which, group]
        return remote(place, place, core_ws.at[w, t], core_wr.at[w, t], sibling)

    def send_line(w):
        for s in range(1, outer):
            start(line_copy(w, s, me, line_peer(s) * inner + p))

    def send_plane(w, t):
        source = line_peer(t) * inner + p
        if t > 0:
            line_copy(w, t, source, me).wait_recv()
        for s in range(1, inner):
            start(plane_copy(w, t, s, source, z * inner + plane_peer(s)))

    def send_near(w):
        for s in range(1, inner):
            source = z * inner + plane_peer(s)
            plane_copy(w, 0, s, source, me).wait_recv()
            start(plane_copy(w, 1, s, source, line_peer(1) * inner + p))
        start(core_copy(w, 0, core))

    def send_core(w):
        for t in range(1, outer):
            for s in range(1, inner):
                source = line_peer(t) * inner + plane_peer(s)
                plane_copy(w, t, s, source, me).wait_recv()
            start(core_copy(w, t, core))

    def finish_weight(w):
        for t in range(outer):
            core_copy(w, t, 1 - core).wait_recv()
        for d in range(count):
            base = d * rows
            rows_f32[base : base + half, :] = gathered[w, 0, d].astype(jnp.float32)
            rows_f32[base + half : base + rows, :] = gathered[w, 1, d].astype(jnp.float32)[
                : rows - half
            ]
        for k in range(27):
            block = rows_f32[k * channels : (k + 1) * channels, :].astype(jnp.bfloat16)
            a, rest = divmod(k, 9)
            weights[w, rest * channels : (rest + 1) * channels, a * channels : (a + 1) * channels] = block
            a, rest = divmod(26 - k, 9)
            turned[w, a * channels : (a + 1) * channels, rest * channels : (rest + 1) * channels] = block

    def spread(cols, values):
        field = values.reshape(depth * height, width, channels)
        place = lax.broadcasted_iota(jnp.int32, field.shape, 1)
        left = jnp.where(place == 0, 0.0, pltpu.roll(field, 1, 1))
        right = jnp.where(place == width - 1, 0.0, pltpu.roll(field, width - 1, 1))
        for c, moved in enumerate((left, field, right)):
            moved = moved.reshape(depth, height, width, channels)
            edge = jnp.zeros((depth, 1, width, channels), jnp.float32)
            for b in range(3):
                if b == 0:
                    piece = jnp.concatenate([edge, moved[:, :-1]], axis=1)
                elif b == 1:
                    piece = moved
                else:
                    piece = jnp.concatenate([moved[:, 1:], edge], axis=1)
                k = 3 * b + c
                cols[:, k * channels : (k + 1) * channels] = piece.reshape(cells, channels).astype(
                    jnp.bfloat16
                )

    edge_plane = jnp.zeros((area, channels), jnp.float32)

    def fold_planes(parts):
        before, here, after = (parts[:, a * channels : (a + 1) * channels] for a in range(3))
        return (
            jnp.concatenate([edge_plane, before[:-area]], axis=0)
            + here
            + jnp.concatenate([after[area:], edge_plane], axis=0)
        )

    def forward(cols, w):
        return fold_planes(jnp.dot(cols[...], weights[w], preferred_element_type=jnp.float32))

    def backward(cols, w):
        return fold_planes(
            lax.dot_general(
                cols[...],
                turned[w],
                (((1,), (1,)), ((), ())),
                preferred_element_type=jnp.float32,
            )
        )

    def normalize(values):
        average = jnp.sum(values, axis=0, keepdims=True) / cells
        square_mean = jnp.sum(values * values, axis=0, keepdims=True) / cells
        inverse = lax.rsqrt(square_mean - average * average + EPSILON)
        return (values - average) * inverse, inverse

    def norm_back(grad, normed, inverse):
        plain = jnp.sum(grad, axis=0, keepdims=True) / cells
        paired = jnp.sum(grad * normed, axis=0, keepdims=True) / cells
        return inverse * (grad - plain - normed * paired)

    def weight_grad(cols, delta, g):
        planes[:, :channels] = jnp.concatenate([delta[area:], edge_plane], axis=0).astype(
            jnp.bfloat16
        )
        planes[:, channels : 2 * channels] = delta.astype(jnp.bfloat16)
        planes[:, 2 * channels :] = jnp.concatenate([edge_plane, delta[:-area]], axis=0).astype(
            jnp.bfloat16
        )
        result = lax.dot_general(
            cols[...], planes[...], (((0,), (0,)), ((), ())), preferred_element_type=jnp.float32
        )
        for a in range(3):
            for rest in range(9):
                k = 9 * a + rest
                grad_rows[g, k * channels : (k + 1) * channels, :] = result[
                    rest * channels : (rest + 1) * channels, a * channels : (a + 1) * channels
                ]
        for s in reversed(range(inner)):
            part = own_part(g, line_peer(1) * inner + plane_peer(s))
            near_send[g, s] = part.astype(jnp.bfloat16)
            start(near_grad_copy(g, s, line_peer(1) * inner + p))
        for t in reversed(range(2, outer)):
            for s in range(1, inner):
                target = plane_peer(s)
                part = own_part(g, line_peer(t) * inner + target)
                grad_send[g, s, t] = part.astype(jnp.bfloat16)
                start(plane_grad_copy(g, s, t, z * inner + target))

    def own_part(g, d):
        offset = pl.multiple_of(d * rows + core * half, 8)
        return grad_rows[g, pl.ds(offset, half), :]

    def near_grad_copy(g, s, target):
        return remote(
            near_send.at[g, s],
            near_recv.at[g, s],
            near_gs.at[g, s],
            near_gr.at[g, s],
            (target, core),
        )

    def plane_grad_copy(g, s, t, target):
        return remote(
            grad_send.at[g, s, t],
            grad_recv.at[g, s, t],
            plane_gs.at[g, s, t],
            plane_gr.at[g, s, t],
            (target, core),
        )

    def line_grad_copy(g, t, target):
        return remote(
            line_send.at[g, t],
            line_recv.at[g, t],
            line_gs.at[g, t],
            line_gr.at[g, t],
            (target, core),
        )

    def core_grad_copy(g, which):
        place = halves.at[g, which]
        return remote(place, place, core_gs.at[g], core_gr.at[g], sibling)

    def reduce_near(g):
        for s in reversed(range(inner)):
            near_grad_copy(g, s, me).wait_recv()
            target = z * inner + plane_peer(s)
            total = own_part(g, target) + near_recv[g, s].astype(jnp.float32)
            if s > 0:
                grad_send[g, s, 0] = total.astype(jnp.bfloat16)
                start(plane_grad_copy(g, s, 0, target))
            else:
                halves[g, core] = total

    def reduce_plane(g):
        for t in reversed(range(2, outer)):
            target = line_peer(t) * inner + p
            total = own_part(g, target)
            for s in range(1, inner):
                plane_grad_copy(g, s, t, me).wait_recv()
                total = total + grad_recv[g, s, t].astype(jnp.float32)
            line_send[g, t] = total.astype(jnp.bfloat16)
            start(line_grad_copy(g, t, target))

    def reduce_line(g):
        total = halves[g, core]
        for s in range(1, inner):
            plane_grad_copy(g, s, 0, me).wait_recv()
            total = total + grad_recv[g, s, 0].astype(jnp.float32)
        for t in range(2, outer):
            line_grad_copy(g, t, me).wait_recv()
            total = total + line_recv[g, t].astype(jnp.float32)
        halves[g, core] = total * factor
        start(core_grad_copy(g, core))

    def write_grad(g, ref):
        core_grad_copy(g, 1 - core).wait_recv()
        ref[0:half, :] = halves[g, 0]
        ref[half:rows, :] = halves[g, 1][: rows - half]

    send_line(0)
    send_line(1)
    send_plane(0, 0)
    send_plane(1, 0)
    own_rows = pl.ds(pl.multiple_of(core * own_cells, own_cells), own_cells)
    other_rows = pl.ds(pl.multiple_of((1 - core) * own_cells, own_cells), own_cells)
    for f, ref in enumerate((image_ref, cotangent_ref)):
        start(
            remote(ref, fields.at[f, own_rows], field_send.at[f], field_recv.at[f], sibling)
        )
        fields[f, own_rows, :] = ref[...]
    line_copy(0, 1, line_peer(1) * inner + p, me).wait_recv()
    send_near(0)
    for t in range(2, outer):
        send_plane(0, t)
    grad_rows[:, count * rows :, :] = jnp.zeros_like(grad_rows[:, count * rows :, :])
    for f, ref in enumerate((image_ref, cotangent_ref)):
        remote(
            ref, fields.at[f, other_rows], field_send.at[f], field_recv.at[f], sibling
        ).wait_recv()
    spread(image_cols, fields[0].astype(jnp.float32))
    send_near(1)
    line_copy(1, 1, line_peer(1) * inner + p, me).wait_recv()
    for t in range(2, outer):
        send_plane(1, t)
    send_core(0)
    finish_weight(0)

    first_norm, first_inverse = normalize(forward(image_cols, 0))
    hidden = gelu_value(first_norm).astype(jnp.bfloat16)
    spread(hidden_cols, hidden.astype(jnp.float32))
    send_core(1)
    finish_weight(1)
    second_norm, second_inverse = normalize(forward(hidden_cols, 1))
    summed = fields[0].astype(jnp.float32) + second_norm
    summed_ref[...] = summed
    outer_grad = fields[1].astype(jnp.float32) * gelu_slope(summed)
    outer_ref[...] = outer_grad
    second_delta = norm_back(outer_grad, second_norm, second_inverse)
    second_delta = second_delta.astype(jnp.bfloat16).astype(jnp.float32)
    weight_grad(hidden_cols, second_delta, 1)
    spread(delta_cols, second_delta)
    inner_grad = backward(delta_cols, 1)
    first_delta = norm_back(inner_grad * gelu_slope(first_norm), first_norm, first_inverse)
    first_delta = first_delta.astype(jnp.bfloat16).astype(jnp.float32)
    weight_grad(image_cols, first_delta, 0)
    spread(delta_cols, first_delta)
    outer_ref[...] = outer_ref[...] + backward(delta_cols, 0)
    image_grad_ref[...] = outer_ref[own_rows, :].astype(jnp.bfloat16)
    output_ref[...] = gelu_value(summed_ref[own_rows, :]).astype(jnp.bfloat16)
    reduce_plane(1)
    reduce_near(1)
    reduce_plane(0)
    reduce_near(0)
    reduce_line(1)
    write_grad(1, second_grad_ref)
    reduce_line(0)
    write_grad(0, first_grad_ref)
    for copy in sends:
        copy.wait_send()


def hand_over(*results):
    def kernel(*refs):
        for source, target in zip(refs[: len(results)], refs[len(results) :]):
            target[...] = source[...]

    whole = pl.BlockSpec(memory_space=pltpu.VMEM)
    return pl.pallas_call(
        kernel,
        out_shape=tuple(jax.ShapeDtypeStruct(x.shape, x.dtype) for x in results),
        in_specs=[whole] * len(results),
        out_specs=(whole,) * len(results),
    )(*results)


def fused(count, image, cotangent, first_weight, second_weight):
    _, depth, height, width, channels = image.shape
    own_cells = depth * height * width
    cells = 2 * own_cells
    rows = first_weight.shape[0]
    half = -(-rows // 32) * 16
    inner = group_size(count)
    outer = count // inner
    sizes = (count, inner, 2 * depth, height, width, channels, rows)
    bf16, f32 = jnp.bfloat16, jnp.float32
    dma = pltpu.SemaphoreType.DMA
    whole = pl.BlockSpec(memory_space=pltpu.VMEM)
    output, image_grad, first_grad, second_grad = pl.pallas_call(
        functools.partial(block_kernel, sizes),
        out_shape=(
            jax.ShapeDtypeStruct((own_cells, channels), bf16),
            jax.ShapeDtypeStruct((own_cells, channels), bf16),
            jax.ShapeDtypeStruct((rows, channels), f32),
            jax.ShapeDtypeStruct((rows, channels), f32),
        ),
        in_specs=[whole] * 4,
        out_specs=(whole,) * 4,
        scratch_shapes=[
            pltpu.VMEM((2, cells, channels), bf16),
            pltpu.VMEM((2, 2, count, half, channels), bf16),
            pltpu.VMEM((27 * channels, channels), f32),
            pltpu.VMEM((2, 9 * channels, 3 * channels), bf16),
            pltpu.VMEM((2, 3 * channels, 9 * channels), bf16),
            pltpu.VMEM((cells, 9 * channels), bf16),
            pltpu.VMEM((cells, 9 * channels), bf16),
            pltpu.VMEM((cells, 9 * channels), bf16),
            pltpu.VMEM((cells, 3 * channels), bf16),
            pltpu.VMEM((2, 27 * channels + 2 * half - rows, channels), f32),
            pltpu.VMEM((2, inner, outer, half, channels), bf16),
            pltpu.VMEM((2, inner, outer, half, channels), bf16),
            pltpu.VMEM((2, inner, half, channels), bf16),
            pltpu.VMEM((2, inner, half, channels), bf16),
            pltpu.VMEM((2, outer, half, channels), bf16),
            pltpu.VMEM((2, outer, half, channels), bf16),
            pltpu.VMEM((2, 2, half, channels), f32),
            pltpu.VMEM((cells, channels), f32),
            pltpu.VMEM((cells, channels), f32),
            dma((2,)),
            dma((2,)),
            dma((2, outer)),
            dma((2, outer)),
            dma((2, outer, inner)),
            dma((2, outer, inner)),
            dma((2, outer)),
            dma((2, outer)),
            dma((2, inner, outer)),
            dma((2, inner, outer)),
            dma((2, inner)),
            dma((2, inner)),
            dma((2, outer)),
            dma((2, outer)),
            dma((2,)),
            dma((2,)),
        ],
        compiler_params=pltpu.CompilerParams(
            collective_id=0, has_side_effects=True, vmem_limit_bytes=56 * 1024 * 1024
        ),
        cost_estimate=pl.CostEstimate(
            flops=12 * cells * 27 * channels * channels,
            bytes_accessed=12 * own_cells * channels,
            transcendentals=6 * cells * channels,
        ),
    )(
        image.reshape(own_cells, channels),
        cotangent.reshape(own_cells, channels),
        first_weight,
        second_weight,
    )
    output, image_grad, first_grad, second_grad = hand_over(
        output, image_grad, first_grad, second_grad
    )
    return output.reshape(image.shape), image_grad.reshape(image.shape), first_grad, second_grad


def fits_kernel(count, slabs, image, first_weight):
    _, depth, height, width, channels = image.shape
    rows = first_weight.shape[0]
    inner = group_size(count)
    return (
        slabs == 2
        and image.shape[0] == 1
        and inner > 1
        and count // inner > 1
        and (count & (count - 1)) == 0
        and width % 8 == 0
        and channels % 128 == 0
        and rows % 8 == 0
        and depth * height * width <= 512
    )


def block(image, cotangent, first_weight, second_weight):
    count, slabs = lax.axis_size("dp"), lax.axis_size("space")
    if fits_kernel(count, slabs, image, first_weight):
        return fused(count, image, cotangent, first_weight, second_weight)
    return local(image, cotangent, first_weight, second_weight)


def solution(mesh):
    return jax.shard_map(
        block,
        mesh=mesh,
        in_specs=(
            P("dp", "space", None, None, None),
            P("dp", "space", None, None, None),
            P("dp", None),
            P("dp", None),
        ),
        out_specs=(
            P("dp", "space", None, None, None),
            P("dp", "space", None, None, None),
            P("dp", None),
            P("dp", None),
        ),
        check_vma=False,
    )
```
